256 devices in a mesh: seq: 64 (over x_hi, y, z), head: 2 (over x_lo), dp: 2 (over core).
Axes of the slice: x: 4 (x_hi: 2, x_lo: 2; x = x_hi * 2 + x_lo), y: 4, z: 8, core: 2. Of those that a mesh axis runs over, the one named last changes fastest.
Arguments:
- queries: bfloat16 [32768, 1792], P(('dp', 'seq'), 'head'), parts along dimension 0, may hold values from -32 to 32
- keys: bfloat16 [32768, 256], P(('dp', 'seq'), 'head'), parts along dimension 0, may hold values from -32 to 32
- values: bfloat16 [32768, 256], P(('dp', 'seq'), 'head'), parts along dimension 0, may hold values from -6 to 6
- doc_ids: int32 [32768], P('dp'), parts along dimension 0, may hold values from 0 to 3, as said below
- block_class: int32 [128, 64], P('dp'), parts along dimension 0, may hold values from 0 to 2, as said below
Outputs:
- attended: bfloat16 [32768, 1792], P(('dp', 'seq'), 'head'), parts along dimension 0
The draws below stay inside these ranges and needn't reach their ends.
There are 2 independent parts, one for each index of `dp`. The reference program is written for one: setup_inputs(seed, part) draws one part's arguments, and reference() takes and returns one part's arrays. A program takes and returns all parts, laid end to end along the dimension named above; each array names one. Nothing has to cross between parts.
Inputs may be any that keep to these rules, and one draw needn't show every extreme that they name: `doc_ids`: document numbers start at 0, never fall along the sequence, rise by one at each change, and change only at positions that are multiples of 64. block_class[a, b] is 1 where a = b, 0 where b > a, and 0 or 2 where b < a; it is 2 where a - b <= 2 or b = 0.
All inputs are finite; a program needn't handle non-finite values.
Results may differ from the reference program's by a relative error of at most 0.008.
Values may be sent and summed in bfloat16 or wider, within the bound.
No kernel may reach another device: no remote copies, remote signals or barrier semaphores. Data moves between devices by JAX's collectives and lax.ppermute only.
A program may use at most 64 MiB of HBM per device.

```python
import math
import jax
import jax.numpy as jnp
from jax import lax

HEAD_SIZE = 128
HQ = 14
KV_HEAD_COUNT = 2
QUERY_PER_KV = 7
TOK_DEV = 256
SEQUENCE_TOKENS = 16384
NBLK = 64


def draw_queries(key, part):
    key = jax.random.fold_in(key, 11)
    starting_sample = jax.random.normal(key, (SEQUENCE_TOKENS, KV_HEAD_COUNT, QUERY_PER_KV, HEAD_SIZE), jnp.float32)
    return starting_sample.reshape(SEQUENCE_TOKENS, HQ * HEAD_SIZE).astype(jnp.bfloat16)


def draw_keys(key, part):
    key = jax.random.fold_in(key, 13)
    starting_sample = jax.random.normal(key, (SEQUENCE_TOKENS, KV_HEAD_COUNT, HEAD_SIZE), jnp.float32)
    return starting_sample.reshape(SEQUENCE_TOKENS, KV_HEAD_COUNT * HEAD_SIZE).astype(jnp.bfloat16)


def draw_doc_ids(key, part):
    key = jax.random.fold_in(key, 5)
    element_total = SEQUENCE_TOKENS // 64
    change_count = SEQUENCE_TOKENS // 6144 + 1
    order = jax.random.permutation(key, element_total - 1).astype(jnp.int32) + 1
    chosen = order[:change_count]
    starts = jnp.zeros((element_total,), jnp.int32).at[chosen].set(1)
    doc_numbers = jnp.cumsum(starts).astype(jnp.int32)
    return jnp.repeat(doc_numbers, 64).astype(jnp.int32)


def draw_block_class(key, part):
    key = jax.random.fold_in(key, 7)
    row_index = jnp.arange(NBLK, dtype=jnp.int32)[:, None]
    column_index = jnp.arange(NBLK, dtype=jnp.int32)[None, :]
    coin_flip = jax.random.randint(key, (NBLK, NBLK), 0, 2) * 2
    lower_part = jnp.where((row_index - column_index <= 2) | (column_index == 0), 2, coin_flip)
    table = jnp.where(row_index == column_index, 1, jnp.where(row_index > column_index, lower_part, 0))
    return table.astype(jnp.int32)


def shard_levels(stream_key, extent, shards, least, largest):
    level, own = 1.0, jax.random.fold_in(stream_key, 6)
    for dim, shards_of in shards:
        draws = jnp.exp(jax.random.uniform(jax.random.fold_in(own, dim), (shards_of,), jnp.float32, least / len(shards), largest / len(shards)))
        level = level * jnp.repeat(draws, extent[dim] // shards_of).reshape([-1 if axis == dim else 1 for axis in range(len(extent))])
    return level


def normal_values(rng, extent, width, reach, cuts=(), kind=jnp.bfloat16):
    loudness = shard_levels(rng, extent, cuts, -0.22, 0.18) if cuts else 1.0
    values = jax.random.normal(rng, extent, jnp.float32) * width * loudness
    return jnp.minimum(jnp.maximum(values, -reach), reach).astype(kind)


def setup_inputs(seed: int = 0, part: int = 0) -> dict:
    arg_keys = jax.random.split(jax.random.key(seed), 6)
    part_keys = jax.random.split(jax.random.fold_in(arg_keys[5], part), 6)
    return {
        "queries": draw_queries(jax.random.fold_in(jax.random.fold_in(arg_keys[5], part), 71), part),
        "keys": draw_keys(jax.random.fold_in(jax.random.fold_in(arg_keys[5], part), 71), part),
        "values": normal_values(part_keys[2], (SEQUENCE_TOKENS, KV_HEAD_COUNT * HEAD_SIZE), 1.0, 6.0, ((0, 64), (1, 2))),
        "doc_ids": draw_doc_ids(jax.random.fold_in(jax.random.fold_in(arg_keys[5], part), 71), part),
        "block_class": draw_block_class(jax.random.fold_in(jax.random.fold_in(arg_keys[5], part), 71), part),
    }


masked_score = -1e+30

def reference(queries, keys, values, doc_ids, block_class):
    length = queries.shape[0]
    key_heads = keys.shape[1] // HEAD_SIZE
    query_rows = min(128, TOK_DEV)
    query_float = queries.astype(jnp.float32).reshape(length, key_heads, -1, HEAD_SIZE)
    key_float = keys.astype(jnp.float32).reshape(length, key_heads, HEAD_SIZE)
    value_float = values.astype(jnp.float32).reshape(length, key_heads, HEAD_SIZE)
    key_pos = jnp.arange(length, dtype=jnp.int32)
    key_block = key_pos // TOK_DEV
    score_scale = 1.0 / math.sqrt(HEAD_SIZE)

    def one_block(block_index):
        first_query = block_index * query_rows
        query_part = lax.dynamic_slice_in_dim(query_float, first_query, query_rows, 0)
        query_pos = first_query + jnp.arange(query_rows, dtype=jnp.int32)
        query_docs = lax.dynamic_slice_in_dim(doc_ids, first_query, query_rows, 0)
        class_rows = jnp.take(block_class, query_pos // TOK_DEV, axis=0)
        class_tile = jnp.take(class_rows, key_block, axis=1)
        allowed = (query_docs[:, None] == doc_ids[None, :]) & ((class_tile == 2) | (class_tile == 1) & (key_pos[None, :] <= query_pos[:, None]))
        scores = jnp.einsum('rhgd,khd->hgrk', query_part, key_float) * score_scale
        scores = jnp.where(allowed, scores, masked_score)
        running_max = lax.optimization_barrier(jnp.max(scores, axis=-1, keepdims=True))
        weights = jnp.where(allowed, jnp.exp(scores - running_max), 0.0)
        totals = lax.optimization_barrier(jnp.sum(weights, axis=-1))
        rounded = lax.optimization_barrier(weights.astype(jnp.bfloat16)).astype(jnp.float32)
        summed = jnp.einsum('hgrk,khd->hgrd', rounded, value_float)
        result = (summed / totals[..., None]).astype(jnp.bfloat16)
        return jnp.transpose(result, (2, 0, 1, 3)).reshape(query_rows, -1)
    blocks = lax.map(one_block, jnp.arange(length // query_rows, dtype=jnp.int32))
    return blocks.reshape(length, -1)
```

```python
import functools
import math

import jax
import jax.numpy as jnp
from jax import lax
from jax.experimental import pallas as pl
from jax.experimental.pallas import tpu as pltpu
from jax.sharding import PartitionSpec as P

HEAD_SIZE = 128
DOC_STEP = 64
ONES_ROWS = 16
SPLIT = 3
SUM_ROWS = HEAD_SIZE + ONES_ROWS
X, Y, Z = 2, 4, 8
PLANE = Y * Z
FAR = Z // 2
DEFERRED = (2, 6, FAR)
ALL_OFFSETS = (0, 1, 7, 2, 6, FAR, 3, 5)
OWN, PARTNER = 0, 1
masked_score = -1e30
least_top = -1e29
SUM_LIMIT = 2.0**100
FACTOR = math.log2(math.e) / math.sqrt(HEAD_SIZE)


def step_kernel(offsets, before, roles, last, held_offsets, class_ref, doc_ref, *refs):
    refs = list(refs)
    columns = {offset: refs.pop(0) for offset in held_offsets if offset != FAR}
    singles = [refs.pop(0) for _ in range(Y if FAR in held_offsets else 0)]
    if before:
        query_t, *state_in = [refs.pop(0) for _ in range(3)]
    else:
        queries = [refs.pop(0) for _ in range(2)]
        query_t = refs.pop(0)
    if last:
        out_ref, buf, value_t, order, masked, query, bias, scores, weights, acc, top, sem = refs
    else:
        acc, top, buf, value_t, order, masked, query, bias, scores, weights, sem = refs
    _, heads, _, rows = query_t.shape
    subs = rows // DOC_STEP
    here = lax.axis_index("seq")
    plane = here // PLANE
    my_y, my_z = here // Z % Y, here % Z
    lane = lax.broadcasted_iota(jnp.int32, (DOC_STEP, rows), 1)

    def query_block(role):
        return here if role == OWN else lax.rem(here + PLANE, X * PLANE)

    def entry(role, offset, dy):
        block = plane * PLANE + (my_y - dy) % Y * Z + (my_z - offset) % Z
        mine = query_block(role)
        used = (class_ref[mine, block] != 0) & (doc_ref[block * subs + subs - 1] >= doc_ref[mine * subs])
        if role == PARTNER:
            used = used & (plane == 0)
        return used, block

    def list_blocks(role, wanted, count, redo=False):
        high = doc_ref[query_block(role) * subs + subs - 1]
        for offset in wanted:
            for dy in range(Y):
                used, block = entry(role, offset, dy)
                if role == OWN and offset in DEFERRED and not redo:
                    used = used & ((plane == 0) if last else (plane != 0))

                @pl.when(used)
                def _():
                    order[count] = block
                    query[count] = role
                    masked[count] = jnp.where(doc_ref[block * subs] == high, 0, 1)

                count = count + used.astype(jnp.int32)
        return count

    def start(step):
        slot = step % 2
        y, z = order[step] // Z % Y, order[step] % Z
        held = (my_y - y) % Y
        away = (my_z - z) % Z
        for offset, ref in columns.items():

            @pl.when(away == offset)
            def _():
                pltpu.make_async_copy(ref.at[held], buf.at[slot], sem.at[slot]).start()

        for dy, ref in enumerate(singles):

            @pl.when((held == dy) & (away == FAR))
            def _():
                pltpu.make_async_copy(ref, buf.at[slot], sem.at[slot]).start()

    def wait(step):
        slot = step % 2
        pltpu.make_async_copy(columns[held_offsets[0]].at[0], buf.at[slot], sem.at[slot]).wait()

    def fill_bias(step, diagonal):
        block = order[step]
        mine = here + query[step] * PLANE
        query_doc = jnp.full((DOC_STEP, rows), doc_ref[mine * subs], jnp.int32)
        for sub in range(1, subs):
            query_doc = jnp.where(lane >= sub * DOC_STEP, doc_ref[mine * subs + sub], query_doc)
        for sub in range(subs):
            allowed = query_doc == doc_ref[block * subs + sub]
            key_row = lax.broadcasted_iota(jnp.int32, (DOC_STEP, rows), 0) + sub * DOC_STEP
            allowed = allowed & ((key_row <= lane) | jnp.logical_not(diagonal))
            bias[sub * DOC_STEP : (sub + 1) * DOC_STEP, :] = jnp.where(allowed, 0.0, masked_score)

    def attend(step, use_bias, first=False, online=False):
        slot = step % 2
        role = query[step]
        key = buf[slot, :rows]
        value_t[:HEAD_SIZE, :] = buf[slot, rows:].T
        for head in range(heads):
            found = jnp.dot(key, query_t[role, head], preferred_element_type=jnp.float32)
            if use_bias:
                found = found + bias[...]
            if first or online:
                scores[head] = found
            else:
                weights[head] = jnp.exp2((found - top[role, head]) * FACTOR).astype(jnp.bfloat16)
        if first or online:
            for head in range(heads):
                best = jnp.maximum(jnp.max(scores[head], axis=0, keepdims=True), least_top)
                if online:
                    earlier = top[role, head]
                    best = jnp.maximum(best, earlier)
                    acc[role, head] = acc[role, head] * jnp.exp2((earlier - best) * FACTOR)
                top[role, head] = best
                weights[head] = jnp.exp2((scores[head] - best) * FACTOR).astype(jnp.bfloat16)
        value = value_t[...]
        for head in range(heads):
            gained = jnp.dot(value, weights[head], preferred_element_type=jnp.float32)
            if first:
                acc[role, head] = gained
            else:
                acc[role, head] = acc[role, head] + gained

    def sweep(count, fresh, online):
        def loop_step(step, carry):
            wait(step)

            @pl.when(step + 1 < count)
            def _():
                start(step + 1)

            role = query[step]
            is_first = step == jnp.where(role == OWN, fresh[OWN], fresh[PARTNER])
            is_masked = is_first | (masked[step] != 0) | online

            @pl.when(is_masked)
            def _():
                fill_bias(step, (order[step] == here) & (role == OWN))

            @pl.when(is_first)
            def _():
                attend(step, True, first=True)

            @pl.when(jnp.logical_not(is_first) & is_masked)
            def _():
                attend(step, True, online=online)

            if not online:

                @pl.when(jnp.logical_not(is_masked))
                def _():
                    attend(step, False)

            return carry

        lax.fori_loop(0, count, loop_step, 0)

    counts = {}
    count = jnp.int32(0)
    fresh = {OWN: jnp.int32(-1), PARTNER: jnp.int32(-1)}
    for role in roles:
        begin = count
        if role == OWN or not before:
            seen = jnp.bool_(bool(before))
        else:
            seen = jnp.bool_(False)
            for offset in before:
                for dy in range(Y):
                    seen = seen | entry(role, offset, dy)[0]
        fresh[role] = jnp.where(seen, -1, begin)
        count = list_blocks(role, offsets, count)

    pl.when(count > 0)(lambda: start(0))
    value_t[HEAD_SIZE:, :] = jnp.ones((ONES_ROWS, rows), jnp.bfloat16)
    for role in roles:
        if before and last:
            acc[role] = state_in[0][role]
            top[role] = state_in[1][role]
        if not before:
            for head in range(heads):
                query_t[role, head] = queries[role][:, head * HEAD_SIZE : (head + 1) * HEAD_SIZE].T
            acc[role] = jnp.zeros(acc.shape[1:], jnp.float32)
            top[role] = jnp.full(top.shape[1:], least_top, jnp.float32)
    sweep(count, fresh, False)
    if not last:
        return

    (role,) = roles
    largest = acc[role, 0, HEAD_SIZE : HEAD_SIZE + 1]
    for head in range(1, heads):
        largest = jnp.maximum(largest, acc[role, head, HEAD_SIZE : HEAD_SIZE + 1])

    @pl.when(jnp.logical_not(jnp.max(largest) <= SUM_LIMIT))
    def _():
        total = list_blocks(role, held_offsets, jnp.int32(0), redo=True)
        start(0)
        sweep(total, {OWN: jnp.int32(0), PARTNER: jnp.int32(0)}, True)

    for head in range(heads):
        out_ref[head, :HEAD_SIZE] = acc[role, head, :HEAD_SIZE].astype(out_ref.dtype)
        stats = []
        for value in (acc[role, head, HEAD_SIZE : HEAD_SIZE + 1], top[role, head]):
            for _ in range(SPLIT):
                part = value.astype(out_ref.dtype).astype(jnp.float32)
                stats.append(part)
                value = value - part
        stats.append(jnp.zeros((ONES_ROWS - 2 * SPLIT, rows), jnp.float32))
        out_ref[head, HEAD_SIZE:] = jnp.concatenate(stats, axis=0).astype(out_ref.dtype)


def merge_kernel(near_ref, far_ref, o_ref):
    has_far = lax.axis_index("seq") // PLANE > 0

    def stats_of(ref, head):
        stats = ref[head, HEAD_SIZE:].astype(jnp.float32)
        total = (stats[2:3] + stats[1:2]) + stats[0:1]
        top = (stats[5:6] + stats[4:5]) + stats[3:4]
        return total, top

    for head in range(near_ref.shape[0]):
        near_total, near_top = stats_of(near_ref, head)
        far_total, far_top = stats_of(far_ref, head)
        far_top = jnp.where(has_far, far_top, least_top)
        best = jnp.maximum(near_top, far_top)
        near = jnp.exp2((near_top - best) * FACTOR)
        far = jnp.exp2((far_top - best) * FACTOR)
        total = near * near_total + far * far_total
        sums = near_ref[head, :HEAD_SIZE] * near + far_ref[head, :HEAD_SIZE].astype(jnp.float32) * far
        o_ref[:, head * HEAD_SIZE : (head + 1) * HEAD_SIZE] = (sums / total).astype(jnp.bfloat16).T


def step(offsets, before, roles, last, tables, columns, singles, state):
    rows = columns[0].shape[1] // 2
    heads = state[0].shape[1] // HEAD_SIZE if not before else state[0].shape[1]
    held = ALL_OFFSETS if last else offsets
    parts = [columns[offset] for offset in held if offset != FAR]
    parts += singles if FAR in held else []
    smem = pl.BlockSpec(memory_space=pltpu.SMEM)
    vmem = pl.BlockSpec(memory_space=pltpu.VMEM)
    task_count = 2 * PLANE
    scratch = [
        pltpu.VMEM((2, 2 * rows, HEAD_SIZE), jnp.bfloat16),
        pltpu.VMEM((SUM_ROWS, rows), jnp.bfloat16),
        pltpu.SMEM((task_count,), jnp.int32),
        pltpu.SMEM((task_count,), jnp.int32),
        pltpu.SMEM((task_count,), jnp.int32),
        pltpu.VMEM((rows, rows), jnp.float32),
        pltpu.VMEM((heads, rows, rows), jnp.float32),
        pltpu.VMEM((heads, rows, rows), jnp.bfloat16),
    ]
    state_shapes = ((2, heads, SUM_ROWS, rows), (2, heads, 1, rows))
    out_shape = [jax.ShapeDtypeStruct(shape, jnp.float32) for shape in state_shapes]
    inputs = (*tables, *parts, *state)
    aliases = {len(inputs) - 2: 0, len(inputs) - 1: 1}
    if last:
        scratch += [pltpu.VMEM(shape, jnp.float32) for shape in state_shapes]
        out_type = jnp.float32 if roles == (OWN,) else jnp.bfloat16
        out_shape, aliases = [jax.ShapeDtypeStruct((heads, SUM_ROWS, rows), out_type)], {}
    elif not before:
        out_shape.insert(0, jax.ShapeDtypeStruct((2, heads, HEAD_SIZE, rows), jnp.bfloat16))
        aliases = {}
    scratch += [pltpu.SemaphoreType.DMA((2,))]
    tasks = len(offsets) * len(roles) * 2
    out = pl.pallas_call(
        functools.partial(step_kernel, offsets, before, roles, last, held),
        out_shape=out_shape,
        in_specs=[smem, smem] + [pl.BlockSpec(memory_space=pl.ANY)] * len(parts) + [vmem] * len(state),
        out_specs=[vmem] * len(out_shape),
        scratch_shapes=scratch,
        input_output_aliases=aliases,
        compiler_params=pltpu.CompilerParams(vmem_limit_bytes=24 * 1024 * 1024),
        cost_estimate=pl.CostEstimate(
            flops=tasks * heads * rows * rows * HEAD_SIZE * 4,
            bytes_accessed=tasks * rows * HEAD_SIZE * 4,
            transcendentals=tasks * heads * rows * rows,
        ),
        name="blocks_" + "".join(str(offset) for offset in offsets) + "_role" + "".join(str(role) for role in roles),
    )(*inputs)
    if last:
        return out[0]
    return tuple(out) if not before else (state[0], *out)


def moved(value, dx, dy, dz, from_planes=range(X)):
    pairs = [
        (((x - dx) % X * Y + (y - dy) % Y) * Z + (z - dz) % Z, (x * Y + y) * Z + z)
        for x in range(X) for y in range(Y) for z in range(Z)
        if (x - dx) % X in from_planes
    ]
    return lax.ppermute(value, "seq", pairs)


def body(queries, keys, values, doc_ids, block_class):
    tables = (block_class, doc_ids.reshape(-1, DOC_STEP)[:, 0])
    both = jnp.concatenate([keys, values], axis=0)
    column = jnp.stack([both] + [moved(both, 0, dy, 0) for dy in range(1, Y)])
    single = moved(both, 0, 0, FAR)
    far_queries = moved(queries, 1, 0, 0)
    column, single = lax.optimization_barrier((column, single))
    columns = {0: column, 1: moved(column, 0, 0, 1), 7: moved(column, 0, 0, -1)}
    singles = [single] + [moved(single, 0, dy, 0) for dy in range(1, Y)]
    both_roles = (OWN, PARTNER)

    state = step((0,), (), both_roles, False, tables, columns, singles, (queries, far_queries))
    columns[1], columns[7], numerators, tops = lax.optimization_barrier((columns[1], columns[7], *state[1:]))
    columns[2], columns[6] = moved(columns[1], 0, 0, 1), moved(columns[7], 0, 0, -1)
    state = step((1, 7), (0,), both_roles, False, tables, columns, singles, (state[0], numerators, tops))
    columns[2], columns[6], *singles, numerators, tops = lax.optimization_barrier(
        (columns[2], columns[6], *singles, *state[1:])
    )
    columns[3], columns[5] = moved(columns[2], 0, 0, 1), moved(columns[6], 0, 0, -1)
    state = step((2, 6, FAR), (0, 1, 7), both_roles, False, tables, columns, singles, (state[0], numerators, tops))
    columns[3], columns[5], numerators, tops = lax.optimization_barrier((columns[3], columns[5], *state[1:]))
    state = (state[0], numerators, tops)
    partner = step((3, 5), (0, 1, 7, 2, 6, FAR), (PARTNER,), True, tables, columns, singles, state)
    partner = moved(partner, 1, 0, 0, (0,))
    own = step((2, 6, FAR, 3, 5), (0, 1, 7), (OWN,), True, tables, columns, singles, state)
    vmem = pl.BlockSpec(memory_space=pltpu.VMEM)
    return pl.pallas_call(
        merge_kernel,
        out_shape=jax.ShapeDtypeStruct(queries.shape, queries.dtype),
        in_specs=[vmem] * 2,
        out_specs=vmem,
        compiler_params=pltpu.CompilerParams(vmem_limit_bytes=24 * 1024 * 1024),
        name="merge",
    )(own, partner)


def solution(mesh):
    in_specs = (
        P(("dp", "seq"), "head"),
        P(("dp", "seq"), "head"),
        P(("dp", "seq"), "head"),
        P("dp"),
        P("dp", None),
    )
    out_specs = P(("dp", "seq"), "head")
    return jax.shard_map(body, mesh=mesh, in_specs=in_specs, out_specs=out_specs, check_vma=False)
```

```python
import functools
import math

import jax
import jax.numpy as jnp
from jax import lax
from jax.experimental import pallas as pl
from jax.experimental.pallas import tpu as pltpu
from jax.sharding import PartitionSpec as P

HEAD_SIZE = 128
DOC_STEP = 64
ONES_ROWS = 16
SPLIT = 3
STAT_ROWS = 48
SUM_ROWS = HEAD_SIZE + ONES_ROWS
X, Y, Z = 2, 4, 8
PLANE = Y * Z
FAR = Z // 2
DEFERRED = (1, 7, 2, 6, FAR)
ALL_OFFSETS = (0, 1, 7, 2, 6, FAR, 3, 5)
OWN, PARTNER = 0, 1
masked_score = -1e30
least_top = -1e29
SUM_LIMIT = 2.0**100
FACTOR = math.log2(math.e) / math.sqrt(HEAD_SIZE)


def step_kernel(offsets, before, roles, last, held_offsets, class_ref, doc_ref, *refs):
    refs = list(refs)
    columns = {offset: refs.pop(0) for offset in held_offsets if offset != FAR}
    singles = [refs.pop(0) for _ in range(Y if FAR in held_offsets else 0)]
    if before:
        query_t, *state_in = [refs.pop(0) for _ in range(3)]
    else:
        queries = [refs.pop(0) for _ in range(2)]
        query_t = refs.pop(0)
    if last:
        out_ref, buf, value_t, order, masked, query, bias, scores, weights, acc, top, sem = refs
    else:
        acc, top, buf, value_t, order, masked, query, bias, scores, weights, sem = refs
    _, heads, _, rows = query_t.shape
    subs = rows // DOC_STEP
    here = lax.axis_index("seq")
    plane = here // PLANE
    my_y, my_z = here // Z % Y, here % Z
    lane = lax.broadcasted_iota(jnp.int32, (DOC_STEP, rows), 1)

    def query_block(role):
        return here if role == OWN else lax.rem(here + PLANE, X * PLANE)

    def entry(role, offset, dy):
        block = plane * PLANE + (my_y - dy) % Y * Z + (my_z - offset) % Z
        mine = query_block(role)
        used = (class_ref[mine, block] != 0) & (doc_ref[block * subs + subs - 1] >= doc_ref[mine * subs])
        if role == PARTNER:
            used = used & (plane == 0)
        return used, block

    def list_blocks(role, wanted, count, redo=False):
        high = doc_ref[query_block(role) * subs + subs - 1]
        for offset in wanted:
            for dy in range(Y):
                used, block = entry(role, offset, dy)
                if role == OWN and offset in DEFERRED and not redo:
                    used = used & ((plane == 0) if last else (plane != 0))

                @pl.when(used)
                def _():
                    order[count] = block
                    query[count] = role
                    masked[count] = jnp.where(doc_ref[block * subs] == high, 0, 1)

                count = count + used.astype(jnp.int32)
        return count

    def start(step):
        slot = step % 2
        y, z = order[step] // Z % Y, order[step] % Z
        held = (my_y - y) % Y
        away = (my_z - z) % Z
        for offset, ref in columns.items():

            @pl.when(away == offset)
            def _():
                pltpu.make_async_copy(ref.at[held], buf.at[slot], sem.at[slot]).start()

        for dy, ref in enumerate(singles):

            @pl.when((held == dy) & (away == FAR))
            def _():
                pltpu.make_async_copy(ref, buf.at[slot], sem.at[slot]).start()

    def wait(step):
        slot = step % 2
        pltpu.make_async_copy(columns[held_offsets[0]].at[0], buf.at[slot], sem.at[slot]).wait()

    def fill_bias(step, diagonal):
        block = order[step]
        mine = here + query[step] * PLANE
        query_doc = jnp.full((DOC_STEP, rows), doc_ref[mine * subs], jnp.int32)
        for sub in range(1, subs):
            query_doc = jnp.where(lane >= sub * DOC_STEP, doc_ref[mine * subs + sub], query_doc)
        for sub in range(subs):
            allowed = query_doc == doc_ref[block * subs + sub]
            key_row = lax.broadcasted_iota(jnp.int32, (DOC_STEP, rows), 0) + sub * DOC_STEP
            allowed = allowed & ((key_row <= lane) | jnp.logical_not(diagonal))
            bias[sub * DOC_STEP : (sub + 1) * DOC_STEP, :] = jnp.where(allowed, 0.0, masked_score)

    def attend(step, use_bias, first=False, online=False):
        slot = step % 2
        role = query[step]
        key = buf[slot, :rows]
        value_t[:HEAD_SIZE, :] = buf[slot, rows:].T
        for head in range(heads):
            found = jnp.dot(key, query_t[role, head], preferred_element_type=jnp.float32)
            if use_bias:
                found = found + bias[...]
            if first or online:
                scores[head] = found
            else:
                weights[head] = jnp.exp2((found - top[role, head]) * FACTOR).astype(jnp.bfloat16)
        if first or online:
            for head in range(heads):
                best = jnp.maximum(jnp.max(scores[head], axis=0, keepdims=True), least_top)
                if online:
                    earlier = top[role, head]
                    best = jnp.maximum(best, earlier)
                    acc[role, head] = acc[role, head] * jnp.exp2((earlier - best) * FACTOR)
                top[role, head] = best
                weights[head] = jnp.exp2((scores[head] - best) * FACTOR).astype(jnp.bfloat16)
        value = value_t[...]
        for head in range(heads):
            gained = jnp.dot(value, weights[head], preferred_element_type=jnp.float32)
            if first:
                acc[role, head] = gained
            else:
                acc[role, head] = acc[role, head] + gained

    def sweep(count, fresh, online):
        def loop_step(step, carry):
            wait(step)

            @pl.when(step + 1 < count)
            def _():
                start(step + 1)

            role = query[step]
            is_first = step == jnp.where(role == OWN, fresh[OWN], fresh[PARTNER])
            is_masked = is_first | (masked[step] != 0) | online

            @pl.when(is_masked)
            def _():
                fill_bias(step, (order[step] == here) & (role == OWN))

            @pl.when(is_first)
            def _():
                attend(step, True, first=True)

            @pl.when(jnp.logical_not(is_first) & is_masked)
            def _():
                attend(step, True, online=online)

            if not online:

                @pl.when(jnp.logical_not(is_masked))
                def _():
                    attend(step, False)

            return carry

        lax.fori_loop(0, count, loop_step, 0)

    counts = {}
    count = jnp.int32(0)
    fresh = {OWN: jnp.int32(-1), PARTNER: jnp.int32(-1)}
    for role in roles:
        begin = count
        if role == OWN or not before:
            seen = jnp.bool_(bool(before))
        else:
            seen = jnp.bool_(False)
            for offset in before:
                for dy in range(Y):
                    seen = seen | entry(role, offset, dy)[0]
        fresh[role] = jnp.where(seen, -1, begin)
        count = list_blocks(role, offsets, count)

    pl.when(count > 0)(lambda: start(0))
    value_t[HEAD_SIZE:, :] = jnp.ones((ONES_ROWS, rows), jnp.bfloat16)
    for role in roles:
        if before and last:
            acc[role] = state_in[0][role]
            top[role] = state_in[1][role]
        if not before:
            for head in range(heads):
                query_t[role, head] = queries[role][:, head * HEAD_SIZE : (head + 1) * HEAD_SIZE].T
            acc[role] = jnp.zeros(acc.shape[1:], jnp.float32)
            top[role] = jnp.full(top.shape[1:], least_top, jnp.float32)
    sweep(count, fresh, False)
    if not last:
        return

    (role,) = roles
    largest = acc[role, 0, HEAD_SIZE : HEAD_SIZE + 1]
    for head in range(1, heads):
        largest = jnp.maximum(largest, acc[role, head, HEAD_SIZE : HEAD_SIZE + 1])

    @pl.when(jnp.logical_not(jnp.max(largest) <= SUM_LIMIT))
    def _():
        total = list_blocks(role, held_offsets, jnp.int32(0), redo=True)
        start(0)
        sweep(total, {OWN: jnp.int32(0), PARTNER: jnp.int32(0)}, True)

    stats = []
    for head in range(heads):
        out_ref[head * HEAD_SIZE : (head + 1) * HEAD_SIZE] = acc[role, head, :HEAD_SIZE].astype(out_ref.dtype)
        for value in (acc[role, head, HEAD_SIZE : HEAD_SIZE + 1], top[role, head]):
            for _ in range(SPLIT):
                part = value.astype(out_ref.dtype).astype(jnp.float32)
                stats.append(part)
                value = value - part
    stats.append(jnp.zeros((STAT_ROWS - len(stats), rows), jnp.float32))
    out_ref[heads * HEAD_SIZE :] = jnp.concatenate(stats, axis=0).astype(out_ref.dtype)


def merge_kernel(near_ref, far_ref, o_ref):
    has_far = lax.axis_index("seq") // PLANE > 0

    heads = (near_ref.shape[0] - STAT_ROWS) // HEAD_SIZE
    near_stats = near_ref[heads * HEAD_SIZE :].astype(jnp.float32)
    far_stats = far_ref[heads * HEAD_SIZE :].astype(jnp.float32)

    def stats_of(stats, head):
        at = 2 * SPLIT * head
        total = (stats[at + 2 : at + 3] + stats[at + 1 : at + 2]) + stats[at : at + 1]
        top = (stats[at + 5 : at + 6] + stats[at + 4 : at + 5]) + stats[at + 3 : at + 4]
        return total, top

    for head in range(heads):
        held = slice(head * HEAD_SIZE, (head + 1) * HEAD_SIZE)
        near_total, near_top = stats_of(near_stats, head)
        far_total, far_top = stats_of(far_stats, head)
        far_top = jnp.where(has_far, far_top, least_top)
        best = jnp.maximum(near_top, far_top)
        near = jnp.exp2((near_top - best) * FACTOR)
        far = jnp.exp2((far_top - best) * FACTOR)
        total = near * near_total + far * far_total
        sums = near_ref[held] * near + far_ref[held].astype(jnp.float32) * far
        o_ref[:, held] = (sums / total).astype(jnp.bfloat16).T


def step(offsets, before, roles, last, tables, columns, singles, state):
    rows = columns[0].shape[1] // 2
    heads = state[0].shape[1] // HEAD_SIZE if not before else state[0].shape[1]
    held = ALL_OFFSETS if last else offsets
    parts = [columns[offset] for offset in held if offset != FAR]
    parts += singles if FAR in held else []
    smem = pl.BlockSpec(memory_space=pltpu.SMEM)
    vmem = pl.BlockSpec(memory_space=pltpu.VMEM)
    task_count = 2 * PLANE
    scratch = [
        pltpu.VMEM((2, 2 * rows, HEAD_SIZE), jnp.bfloat16),
        pltpu.VMEM((SUM_ROWS, rows), jnp.bfloat16),
        pltpu.SMEM((task_count,), jnp.int32),
        pltpu.SMEM((task_count,), jnp.int32),
        pltpu.SMEM((task_count,), jnp.int32),
        pltpu.VMEM((rows, rows), jnp.float32),
        pltpu.VMEM((heads, rows, rows), jnp.float32),
        pltpu.VMEM((heads, rows, rows), jnp.bfloat16),
    ]
    state_shapes = ((2, heads, SUM_ROWS, rows), (2, heads, 1, rows))
    out_shape = [jax.ShapeDtypeStruct(shape, jnp.float32) for shape in state_shapes]
    inputs = (*tables, *parts, *state)
    aliases = {len(inputs) - 2: 0, len(inputs) - 1: 1}
    if last:
        scratch += [pltpu.VMEM(shape, jnp.float32) for shape in state_shapes]
        out_type = jnp.float32 if roles == (OWN,) else jnp.bfloat16
        out_shape, aliases = [jax.ShapeDtypeStruct((heads * HEAD_SIZE + STAT_ROWS, rows), out_type)], {}
    elif not before:
        out_shape.insert(0, jax.ShapeDtypeStruct((2, heads, HEAD_SIZE, rows), jnp.bfloat16))
        aliases = {}
    scratch += [pltpu.SemaphoreType.DMA((2,))]
    tasks = len(offsets) * len(roles) * 2
    out = pl.pallas_call(
        functools.partial(step_kernel, offsets, before, roles, last, held),
        out_shape=out_shape,
        in_specs=[smem, smem] + [pl.BlockSpec(memory_space=pl.ANY)] * len(parts) + [vmem] * len(state),
        out_specs=[vmem] * len(out_shape),
        scratch_shapes=scratch,
        input_output_aliases=aliases,
        compiler_params=pltpu.CompilerParams(vmem_limit_bytes=24 * 1024 * 1024),
        cost_estimate=pl.CostEstimate(
            flops=tasks * heads * rows * rows * HEAD_SIZE * 4,
            bytes_accessed=tasks * rows * HEAD_SIZE * 4,
            transcendentals=tasks * heads * rows * rows,
        ),
        name="blocks_" + "".join(str(offset) for offset in offsets) + "_role" + "".join(str(role) for role in roles),
    )(*inputs)
    if last:
        return out[0]
    return tuple(out) if not before else (state[0], *out)


def moved(value, dx, dy, dz, from_planes=range(X)):
    pairs = [
        (((x - dx) % X * Y + (y - dy) % Y) * Z + (z - dz) % Z, (x * Y + y) * Z + z)
        for x in range(X) for y in range(Y) for z in range(Z)
        if (x - dx) % X in from_planes
    ]
    return lax.ppermute(value, "seq", pairs)


def body(queries, keys, values, doc_ids, block_class):
    tables = (block_class, doc_ids.reshape(-1, DOC_STEP)[:, 0])
    both = jnp.concatenate([keys, values], axis=0)
    *others, single = lax.optimization_barrier(
        (*[moved(both, 0, dy, 0) for dy in range(1, Y)], moved(both, 0, 0, FAR))
    )
    column = jnp.stack([both, *others])
    far_queries = moved(queries, 1, 0, 0)
    columns = {0: column, 1: moved(column, 0, 0, 1), 7: moved(column, 0, 0, -1)}
    singles = [single] + [moved(single, 0, dy, 0) for dy in range(1, Y)]
    both_roles = (OWN, PARTNER)

    state = step((0,), (), both_roles, False, tables, columns, singles, (queries, far_queries))
    columns[1], columns[7], numerators, tops = lax.optimization_barrier((columns[1], columns[7], *state[1:]))
    columns[2], columns[6] = moved(columns[1], 0, 0, 1), moved(columns[7], 0, 0, -1)
    state = step((1, 7), (0,), both_roles, False, tables, columns, singles, (state[0], numerators, tops))
    columns[2], columns[6], *singles, numerators, tops = lax.optimization_barrier(
        (columns[2], columns[6], *singles, *state[1:])
    )
    columns[3], columns[5] = moved(columns[2], 0, 0, 1), moved(columns[6], 0, 0, -1)
    state = step((2, 6, FAR), (0, 1, 7), both_roles, False, tables, columns, singles, (state[0], numerators, tops))
    columns[3], columns[5], numerators, tops = lax.optimization_barrier((columns[3], columns[5], *state[1:]))
    state = (state[0], numerators, tops)
    partner = step((3, 5), (0, 1, 7, 2, 6, FAR), (PARTNER,), True, tables, columns, singles, state)
    partner = moved(partner, 1, 0, 0, (0,))
    own = step((*DEFERRED, 3, 5), (0,), (OWN,), True, tables, columns, singles, state)
    vmem = pl.BlockSpec(memory_space=pltpu.VMEM)
    return pl.pallas_call(
        merge_kernel,
        out_shape=jax.ShapeDtypeStruct(queries.shape, queries.dtype),
        in_specs=[vmem] * 2,
        out_specs=vmem,
        compiler_params=pltpu.CompilerParams(vmem_limit_bytes=24 * 1024 * 1024),
        name="merge",
    )(own, partner)


def solution(mesh):
    in_specs = (
        P(("dp", "seq"), "head"),
        P(("dp", "seq"), "head"),
        P(("dp", "seq"), "head"),
        P("dp"),
        P("dp", None),
    )
    out_specs = P(("dp", "seq"), "head")
    return jax.shard_map(body, mesh=mesh, in_specs=in_specs, out_specs=out_specs, check_vma=False)
```

```python
import functools
import math

import jax
import jax.numpy as jnp
from jax import lax
from jax.experimental import pallas as pl
from jax.experimental.pallas import tpu as pltpu
from jax.sharding import PartitionSpec as P

HEAD_SIZE = 128
DOC_STEP = 64
ONES_ROWS = 16
SPLIT = 3
STAT_ROWS = 48
SUM_ROWS = HEAD_SIZE + ONES_ROWS
X, Y, Z = 2, 4, 8
PLANE = Y * Z
FAR = Z // 2
STEPS = {(1, 7): 5, (2, 6, FAR): 9}
ALL_OFFSETS = (0, 1, 7, 2, 6, FAR, 3, 5)
OWN, PARTNER = 0, 1
masked_score = -1e30
least_top = -1e29
SUM_LIMIT = 2.0**100
FACTOR = math.log2(math.e) / math.sqrt(HEAD_SIZE)


def step_kernel(offsets, before, roles, last, held_offsets, class_ref, doc_ref, *refs):
    refs = list(refs)
    columns = {offset: refs.pop(0) for offset in held_offsets if offset != FAR}
    singles = [refs.pop(0) for _ in range(Y if FAR in held_offsets else 0)]
    if before:
        query_t, *state_in = [refs.pop(0) for _ in range(3)]
    else:
        queries = [refs.pop(0) for _ in range(2)]
        query_t = refs.pop(0)
    if last:
        out_ref, buf, value_t, order, masked, query, bias, scores, weights, acc, top, sem = refs
    else:
        acc, top, buf, value_t, order, masked, query, bias, scores, weights, sem = refs
    _, heads, _, rows = query_t.shape
    subs = rows // DOC_STEP
    here = lax.axis_index("seq")
    plane = here // PLANE
    my_y, my_z = here // Z % Y, here % Z
    lane = lax.broadcasted_iota(jnp.int32, (DOC_STEP, rows), 1)

    def query_block(role):
        return here if role == OWN else lax.rem(here + PLANE, X * PLANE)

    def entry(role, offset, dy):
        block = plane * PLANE + (my_y - dy) % Y * Z + (my_z - offset) % Z
        mine = query_block(role)
        used = (class_ref[mine, block] != 0) & (doc_ref[block * subs + subs - 1] >= doc_ref[mine * subs])
        if role == PARTNER:
            used = used & (plane == 0)
        return used, block

    put_off = {}
    for group, room in STEPS.items():
        if OWN in roles and group[0] in offsets:
            total = jnp.int32(0)
            for role in (OWN, PARTNER):
                for offset in group:
                    for dy in range(Y):
                        total = total + entry(role, offset, dy)[0].astype(jnp.int32)
            put_off[group] = (plane == 0) & (total > room)

    def list_blocks(role, wanted, count, redo=False):
        high = doc_ref[query_block(role) * subs + subs - 1]
        for offset in wanted:
            for dy in range(Y):
                used, block = entry(role, offset, dy)
                for group, late in put_off.items():
                    if role == OWN and offset in group and not redo:
                        used = used & (late if last else jnp.logical_not(late))

                @pl.when(used)
                def _():
                    order[count] = block
                    query[count] = role
                    masked[count] = jnp.where(doc_ref[block * subs] == high, 0, 1)

                count = count + used.astype(jnp.int32)
        return count

    def start(step):
        slot = step % 2
        y, z = order[step] // Z % Y, order[step] % Z
        held = (my_y - y) % Y
        away = (my_z - z) % Z
        for offset, ref in columns.items():

            @pl.when(away == offset)
            def _():
                pltpu.make_async_copy(ref.at[held], buf.at[slot], sem.at[slot]).start()

        for dy, ref in enumerate(singles):

            @pl.when((held == dy) & (away == FAR))
            def _():
                pltpu.make_async_copy(ref, buf.at[slot], sem.at[slot]).start()

    def wait(step):
        slot = step % 2
        pltpu.make_async_copy(columns[held_offsets[0]].at[0], buf.at[slot], sem.at[slot]).wait()

    def fill_bias(step, diagonal):
        block = order[step]
        mine = here + query[step] * PLANE
        query_doc = jnp.full((DOC_STEP, rows), doc_ref[mine * subs], jnp.int32)
        for sub in range(1, subs):
            query_doc = jnp.where(lane >= sub * DOC_STEP, doc_ref[mine * subs + sub], query_doc)
        for sub in range(subs):
            allowed = query_doc == doc_ref[block * subs + sub]
            key_row = lax.broadcasted_iota(jnp.int32, (DOC_STEP, rows), 0) + sub * DOC_STEP
            allowed = allowed & ((key_row <= lane) | jnp.logical_not(diagonal))
            bias[sub * DOC_STEP : (sub + 1) * DOC_STEP, :] = jnp.where(allowed, 0.0, masked_score)

    def attend(step, use_bias, first=False, online=False):
        slot = step % 2
        role = query[step]
        key = buf[slot, :rows]
        value_t[:HEAD_SIZE, :] = buf[slot, rows:].T
        for head in range(heads):
            found = jnp.dot(key, query_t[role, head], preferred_element_type=jnp.float32)
            if use_bias:
                found = found + bias[...]
            if first or online:
                scores[head] = found
            else:
                weights[head] = jnp.exp2((found - top[role, head]) * FACTOR).astype(jnp.bfloat16)
        if first or online:
            for head in range(heads):
                best = jnp.maximum(jnp.max(scores[head], axis=0, keepdims=True), least_top)
                if online:
                    earlier = top[role, head]
                    best = jnp.maximum(best, earlier)
                    acc[role, head] = acc[role, head] * jnp.exp2((earlier - best) * FACTOR)
                top[role, head] = best
                weights[head] = jnp.exp2((scores[head] - best) * FACTOR).astype(jnp.bfloat16)
        value = value_t[...]
        for head in range(heads):
            gained = jnp.dot(value, weights[head], preferred_element_type=jnp.float32)
            if first:
                acc[role, head] = gained
            else:
                acc[role, head] = acc[role, head] + gained

    def sweep(count, fresh, online):
        def loop_step(step, carry):
            wait(step)

            @pl.when(step + 1 < count)
            def _():
                start(step + 1)

            role = query[step]
            is_first = step == jnp.where(role == OWN, fresh[OWN], fresh[PARTNER])
            is_masked = is_first | (masked[step] != 0) | online

            @pl.when(is_masked)
            def _():
                fill_bias(step, (order[step] == here) & (role == OWN))

            @pl.when(is_first)
            def _():
                attend(step, True, first=True)

            @pl.when(jnp.logical_not(is_first) & is_masked)
            def _():
                attend(step, True, online=online)

            if not online:

                @pl.when(jnp.logical_not(is_masked))
                def _():
                    attend(step, False)

            return carry

        lax.fori_loop(0, count, loop_step, 0)

    counts = {}
    count = jnp.int32(0)
    fresh = {OWN: jnp.int32(-1), PARTNER: jnp.int32(-1)}
    for role in roles:
        begin = count
        if role == OWN or not before:
            seen = jnp.bool_(bool(before))
        else:
            seen = jnp.bool_(False)
            for offset in before:
                for dy in range(Y):
                    seen = seen | entry(role, offset, dy)[0]
        fresh[role] = jnp.where(seen, -1, begin)
        count = list_blocks(role, offsets, count)

    pl.when(count > 0)(lambda: start(0))
    value_t[HEAD_SIZE:, :] = jnp.ones((ONES_ROWS, rows), jnp.bfloat16)
    for role in roles:
        if before and last:
            acc[role] = state_in[0][role]
            top[role] = state_in[1][role]
        if not before:
            for head in range(heads):
                query_t[role, head] = queries[role][:, head * HEAD_SIZE : (head + 1) * HEAD_SIZE].T
            acc[role] = jnp.zeros(acc.shape[1:], jnp.float32)
            top[role] = jnp.full(top.shape[1:], least_top, jnp.float32)
    sweep(count, fresh, False)
    if not last:
        return

    (role,) = roles
    largest = acc[role, 0, HEAD_SIZE : HEAD_SIZE + 1]
    for head in range(1, heads):
        largest = jnp.maximum(largest, acc[role, head, HEAD_SIZE : HEAD_SIZE + 1])

    @pl.when(jnp.logical_not(jnp.max(largest) <= SUM_LIMIT))
    def _():
        total = list_blocks(role, held_offsets, jnp.int32(0), redo=True)
        start(0)
        sweep(total, {OWN: jnp.int32(0), PARTNER: jnp.int32(0)}, True)

    stats = []
    for head in range(heads):
        out_ref[head * HEAD_SIZE : (head + 1) * HEAD_SIZE] = acc[role, head, :HEAD_SIZE].astype(out_ref.dtype)
        for value in (acc[role, head, HEAD_SIZE : HEAD_SIZE + 1], top[role, head]):
            for _ in range(SPLIT):
                part = value.astype(out_ref.dtype).astype(jnp.float32)
                stats.append(part)
                value = value - part
    stats.append(jnp.zeros((STAT_ROWS - len(stats), rows), jnp.float32))
    out_ref[heads * HEAD_SIZE :] = jnp.concatenate(stats, axis=0).astype(out_ref.dtype)


def merge_kernel(near_ref, far_ref, o_ref):
    has_far = lax.axis_index("seq") // PLANE > 0

    heads = (near_ref.shape[0] - STAT_ROWS) // HEAD_SIZE
    near_stats = near_ref[heads * HEAD_SIZE :].astype(jnp.float32)
    far_stats = far_ref[heads * HEAD_SIZE :].astype(jnp.float32)

    def stats_of(stats, head):
        at = 2 * SPLIT * head
        total = (stats[at + 2 : at + 3] + stats[at + 1 : at + 2]) + stats[at : at + 1]
        top = (stats[at + 5 : at + 6] + stats[at + 4 : at + 5]) + stats[at + 3 : at + 4]
        return total, top

    for head in range(heads):
        held = slice(head * HEAD_SIZE, (head + 1) * HEAD_SIZE)
        near_total, near_top = stats_of(near_stats, head)
        far_total, far_top = stats_of(far_stats, head)
        far_top = jnp.where(has_far, far_top, least_top)
        best = jnp.maximum(near_top, far_top)
        near = jnp.exp2((near_top - best) * FACTOR)
        far = jnp.exp2((far_top - best) * FACTOR)
        total = near * near_total + far * far_total
        sums = near_ref[held] * near + far_ref[held].astype(jnp.float32) * far
        o_ref[:, held] = (sums / total).astype(jnp.bfloat16).T


def step(offsets, before, roles, last, tables, columns, singles, state):
    rows = columns[0].shape[1] // 2
    heads = state[0].shape[1] // HEAD_SIZE if not before else state[0].shape[1]
    held = ALL_OFFSETS if last else offsets
    parts = [columns[offset] for offset in held if offset != FAR]
    parts += singles if FAR in held else []
    smem = pl.BlockSpec(memory_space=pltpu.SMEM)
    vmem = pl.BlockSpec(memory_space=pltpu.VMEM)
    task_count = 2 * PLANE
    scratch = [
        pltpu.VMEM((2, 2 * rows, HEAD_SIZE), jnp.bfloat16),
        pltpu.VMEM((SUM_ROWS, rows), jnp.bfloat16),
        pltpu.SMEM((task_count,), jnp.int32),
        pltpu.SMEM((task_count,), jnp.int32),
        pltpu.SMEM((task_count,), jnp.int32),
        pltpu.VMEM((rows, rows), jnp.float32),
        pltpu.VMEM((heads, rows, rows), jnp.float32),
        pltpu.VMEM((heads, rows, rows), jnp.bfloat16),
    ]
    state_shapes = ((2, heads, SUM_ROWS, rows), (2, heads, 1, rows))
    out_shape = [jax.ShapeDtypeStruct(shape, jnp.float32) for shape in state_shapes]
    inputs = (*tables, *parts, *state)
    aliases = {len(inputs) - 2: 0, len(inputs) - 1: 1}
    if last:
        scratch += [pltpu.VMEM(shape, jnp.float32) for shape in state_shapes]
        out_type = jnp.float32 if roles == (OWN,) else jnp.bfloat16
        out_shape, aliases = [jax.ShapeDtypeStruct((heads * HEAD_SIZE + STAT_ROWS, rows), out_type)], {}
    elif not before:
        out_shape.insert(0, jax.ShapeDtypeStruct((2, heads, HEAD_SIZE, rows), jnp.bfloat16))
        aliases = {}
    scratch += [pltpu.SemaphoreType.DMA((2,))]
    tasks = len(offsets) * len(roles) * 2
    out = pl.pallas_call(
        functools.partial(step_kernel, offsets, before, roles, last, held),
        out_shape=out_shape,
        in_specs=[smem, smem] + [pl.BlockSpec(memory_space=pl.ANY)] * len(parts) + [vmem] * len(state),
        out_specs=[vmem] * len(out_shape),
        scratch_shapes=scratch,
        input_output_aliases=aliases,
        compiler_params=pltpu.CompilerParams(vmem_limit_bytes=24 * 1024 * 1024),
        cost_estimate=pl.CostEstimate(
            flops=tasks * heads * rows * rows * HEAD_SIZE * 4,
            bytes_accessed=tasks * rows * HEAD_SIZE * 4,
            transcendentals=tasks * heads * rows * rows,
        ),
        name="blocks_" + "".join(str(offset) for offset in offsets) + "_role" + "".join(str(role) for role in roles),
    )(*inputs)
    if last:
        return out[0]
    return tuple(out) if not before else (state[0], *out)


def moved(value, dx, dy, dz, from_planes=range(X)):
    pairs = [
        (((x - dx) % X * Y + (y - dy) % Y) * Z + (z - dz) % Z, (x * Y + y) * Z + z)
        for x in range(X) for y in range(Y) for z in range(Z)
        if (x - dx) % X in from_planes
    ]
    return lax.ppermute(value, "seq", pairs)


def body(queries, keys, values, doc_ids, block_class):
    tables = (block_class, doc_ids.reshape(-1, DOC_STEP)[:, 0])
    both = jnp.concatenate([keys, values], axis=0)
    column = jnp.stack([both] + [moved(both, 0, dy, 0) for dy in range(1, Y)])
    single = moved(both, 0, 0, FAR)
    column, single = lax.optimization_barrier((column, single))
    far_queries = moved(queries, 1, 0, 0)
    columns = {0: column, 1: moved(column, 0, 0, 1), 7: moved(column, 0, 0, -1)}
    singles = [single] + [moved(single, 0, dy, 0) for dy in range(1, Y)]
    both_roles = (OWN, PARTNER)

    state = step((0,), (), both_roles, False, tables, columns, singles, (queries, far_queries))
    columns[1], columns[7], numerators, tops = lax.optimization_barrier((columns[1], columns[7], *state[1:]))
    columns[2], columns[6] = moved(columns[1], 0, 0, 1), moved(columns[7], 0, 0, -1)
    state = step((1, 7), (0,), both_roles, False, tables, columns, singles, (state[0], numerators, tops))
    columns[2], columns[6], *singles, numerators, tops = lax.optimization_barrier(
        (columns[2], columns[6], *singles, *state[1:])
    )
    columns[3], columns[5] = moved(columns[2], 0, 0, 1), moved(columns[6], 0, 0, -1)
    state = step((2, 6, FAR), (0, 1, 7), both_roles, False, tables, columns, singles, (state[0], numerators, tops))
    columns[3], columns[5], numerators, tops = lax.optimization_barrier((columns[3], columns[5], *state[1:]))
    state = (state[0], numerators, tops)
    partner = step((3, 5), (0, 1, 7, 2, 6, FAR), (PARTNER,), True, tables, columns, singles, state)
    partner = moved(partner, 1, 0, 0, (0,))
    own = step((1, 7, 2, 6, FAR, 3, 5), (0,), (OWN,), True, tables, columns, singles, state)
    vmem = pl.BlockSpec(memory_space=pltpu.VMEM)
    return pl.pallas_call(
        merge_kernel,
        out_shape=jax.ShapeDtypeStruct(queries.shape, queries.dtype),
        in_specs=[vmem] * 2,
        out_specs=vmem,
        compiler_params=pltpu.CompilerParams(vmem_limit_bytes=24 * 1024 * 1024),
        name="merge",
    )(own, partner)


def solution(mesh):
    in_specs = (
        P(("dp", "seq"), "head"),
        P(("dp", "seq"), "head"),
        P(("dp", "seq"), "head"),
        P("dp"),
        P("dp", None),
    )
    out_specs = P(("dp", "seq"), "head")
    return jax.shard_map(body, mesh=mesh, in_specs=in_specs, out_specs=out_specs, check_vma=False)
```

```python
import functools
import math

import jax
import jax.numpy as jnp
from jax import lax
from jax.experimental import pallas as pl
from jax.experimental.pallas import tpu as pltpu
from jax.sharding import PartitionSpec as P

HEAD_SIZE = 128
DOC_STEP = 64
ONES_ROWS = 16
SPLIT = 3
STAT_ROWS = 48
SUM_ROWS = HEAD_SIZE + ONES_ROWS
X, Y, Z = 2, 4, 8
PLANE = Y * Z
FAR = Z // 2
STEPS = {(1, 7): 5, (2, 6, FAR): 9}
ALL_OFFSETS = (0, 1, 7, 2, 6, FAR, 3, 5)
OWN, PARTNER = 0, 1
masked_score = -1e30
least_top = -1e29
SUM_LIMIT = 2.0**100
FACTOR = math.log2(math.e) / math.sqrt(HEAD_SIZE)


def step_kernel(offsets, before, roles, last, held_offsets, class_ref, doc_ref, *refs):
    refs = list(refs)
    columns = {offset: refs.pop(0) for offset in held_offsets if offset != FAR}
    singles = [refs.pop(0) for _ in range(Y if FAR in held_offsets else 0)]
    if before:
        query_t, *state_in = [refs.pop(0) for _ in range(3)]
    else:
        queries = [refs.pop(0) for _ in range(2)]
        query_t = refs.pop(0)
    if last:
        out_ref, buf, value_t, order, masked, query, bias, scores, weights, acc, top, sem = refs
    else:
        acc, top, buf, value_t, order, masked, query, bias, scores, weights, sem = refs
    _, heads, _, rows = query_t.shape
    subs = rows // DOC_STEP
    here = lax.axis_index("seq")
    plane = here // PLANE
    my_y, my_z = here // Z % Y, here % Z
    lane = lax.broadcasted_iota(jnp.int32, (DOC_STEP, rows), 1)

    def query_block(role):
        return here if role == OWN else lax.rem(here + PLANE, X * PLANE)

    def entry(role, offset, dy):
        block = plane * PLANE + (my_y - dy) % Y * Z + (my_z - offset) % Z
        mine = query_block(role)
        used = (class_ref[mine, block] != 0) & (doc_ref[block * subs + subs - 1] >= doc_ref[mine * subs])
        if role == PARTNER:
            used = used & (plane == 0)
        return used, block

    put_off = {}
    for group, room in STEPS.items():
        if OWN in roles and group[0] in offsets:
            total = jnp.int32(0)
            for role in (OWN, PARTNER):
                for offset in group:
                    for dy in range(Y):
                        total = total + entry(role, offset, dy)[0].astype(jnp.int32)
            put_off[group] = (plane == 0) & (total > room)

    def list_blocks(role, wanted, count, redo=False):
        high = doc_ref[query_block(role) * subs + subs - 1]
        for offset in wanted:
            for dy in range(Y):
                used, block = entry(role, offset, dy)
                for group, late in put_off.items():
                    if role == OWN and offset in group and not redo:
                        used = used & (late if last else jnp.logical_not(late))

                @pl.when(used)
                def _():
                    order[count] = block
                    query[count] = role
                    masked[count] = jnp.where(doc_ref[block * subs] == high, 0, 1)

                count = count + used.astype(jnp.int32)
        return count

    def start(step):
        slot = step % 2
        y, z = order[step] // Z % Y, order[step] % Z
        held = (my_y - y) % Y
        away = (my_z - z) % Z
        for offset, ref in columns.items():

            @pl.when(away == offset)
            def _():
                pltpu.make_async_copy(ref.at[held], buf.at[slot], sem.at[slot]).start()

        for dy, ref in enumerate(singles):

            @pl.when((held == dy) & (away == FAR))
            def _():
                pltpu.make_async_copy(ref, buf.at[slot], sem.at[slot]).start()

    def wait(step):
        slot = step % 2
        pltpu.make_async_copy(columns[held_offsets[0]].at[0], buf.at[slot], sem.at[slot]).wait()

    def fill_bias(step, diagonal):
        block = order[step]
        mine = here + query[step] * PLANE
        query_doc = jnp.full((DOC_STEP, rows), doc_ref[mine * subs], jnp.int32)
        for sub in range(1, subs):
            query_doc = jnp.where(lane >= sub * DOC_STEP, doc_ref[mine * subs + sub], query_doc)
        for sub in range(subs):
            allowed = query_doc == doc_ref[block * subs + sub]
            key_row = lax.broadcasted_iota(jnp.int32, (DOC_STEP, rows), 0) + sub * DOC_STEP
            allowed = allowed & ((key_row <= lane) | jnp.logical_not(diagonal))
            bias[sub * DOC_STEP : (sub + 1) * DOC_STEP, :] = jnp.where(allowed, 0.0, masked_score)

    def attend(step, use_bias, first=False, online=False):
        slot = step % 2
        role = query[step]
        key = buf[slot, :rows]
        value_t[:HEAD_SIZE, :] = buf[slot, rows:].T
        for head in range(heads):
            found = jnp.dot(key, query_t[role, head], preferred_element_type=jnp.float32)
            if use_bias:
                found = found + bias[...]
            if first or online:
                scores[head] = found
            else:
                weights[head] = jnp.exp2((found - top[role, head]) * FACTOR).astype(jnp.bfloat16)
        if first or online:
            for head in range(heads):
                best = jnp.maximum(jnp.max(scores[head], axis=0, keepdims=True), least_top)
                if online:
                    earlier = top[role, head]
                    best = jnp.maximum(best, earlier)
                    acc[role, head] = acc[role, head] * jnp.exp2((earlier - best) * FACTOR)
                top[role, head] = best
                weights[head] = jnp.exp2((scores[head] - best) * FACTOR).astype(jnp.bfloat16)
        value = value_t[...]
        for head in range(heads):
            gained = jnp.dot(value, weights[head], preferred_element_type=jnp.float32)
            if first:
                acc[role, head] = gained
            else:
                acc[role, head] = acc[role, head] + gained

    def sweep(count, fresh, online):
        def loop_step(step, carry):
            wait(step)

            @pl.when(step + 1 < count)
            def _():
                start(step + 1)

            role = query[step]
            is_first = step == jnp.where(role == OWN, fresh[OWN], fresh[PARTNER])
            is_masked = is_first | (masked[step] != 0) | online

            @pl.when(is_masked)
            def _():
                fill_bias(step, (order[step] == here) & (role == OWN))

            @pl.when(is_first)
            def _():
                attend(step, True, first=True)

            @pl.when(jnp.logical_not(is_first) & is_masked)
            def _():
                attend(step, True, online=online)

            if not online:

                @pl.when(jnp.logical_not(is_masked))
                def _():
                    attend(step, False)

            return carry

        lax.fori_loop(0, count, loop_step, 0)

    counts = {}
    count = jnp.int32(0)
    fresh = {OWN: jnp.int32(-1), PARTNER: jnp.int32(-1)}
    for role in roles:
        begin = count
        if role == OWN or not before:
            seen = jnp.bool_(bool(before))
        else:
            seen = jnp.bool_(False)
            for offset in before:
                for dy in range(Y):
                    seen = seen | entry(role, offset, dy)[0]
        fresh[role] = jnp.where(seen, -1, begin)
        count = list_blocks(role, offsets, count)

    pl.when(count > 0)(lambda: start(0))
    value_t[HEAD_SIZE:, :] = jnp.ones((ONES_ROWS, rows), jnp.bfloat16)
    for role in roles:
        if before and last:
            acc[role] = state_in[0][role]
            top[role] = state_in[1][role]
        if not before:
            for head in range(heads):
                query_t[role, head] = queries[role][:, head * HEAD_SIZE : (head + 1) * HEAD_SIZE].T
            acc[role] = jnp.zeros(acc.shape[1:], jnp.float32)
            top[role] = jnp.full(top.shape[1:], least_top, jnp.float32)
    sweep(count, fresh, False)
    if not last:
        return

    (role,) = roles
    largest = acc[role, 0, HEAD_SIZE : HEAD_SIZE + 1]
    for head in range(1, heads):
        largest = jnp.maximum(largest, acc[role, head, HEAD_SIZE : HEAD_SIZE + 1])

    @pl.when(jnp.logical_not(jnp.max(largest) <= SUM_LIMIT))
    def _():
        total = list_blocks(role, held_offsets, jnp.int32(0), redo=True)
        start(0)
        sweep(total, {OWN: jnp.int32(0), PARTNER: jnp.int32(0)}, True)

    stats = []
    for head in range(heads):
        out_ref[head * HEAD_SIZE : (head + 1) * HEAD_SIZE] = acc[role, head, :HEAD_SIZE].astype(out_ref.dtype)
        for value in (acc[role, head, HEAD_SIZE : HEAD_SIZE + 1], top[role, head]):
            for _ in range(SPLIT):
                part = value.astype(out_ref.dtype).astype(jnp.float32)
                stats.append(part)
                value = value - part
    stats.append(jnp.zeros((STAT_ROWS - len(stats), rows), jnp.float32))
    out_ref[heads * HEAD_SIZE :] = jnp.concatenate(stats, axis=0).astype(out_ref.dtype)


def merge_kernel(near_ref, far_ref, o_ref):
    has_far = lax.axis_index("seq") // PLANE > 0

    heads = (near_ref.shape[0] - STAT_ROWS) // HEAD_SIZE
    near_stats = near_ref[heads * HEAD_SIZE :].astype(jnp.float32)
    far_stats = far_ref[heads * HEAD_SIZE :].astype(jnp.float32)

    def stats_of(stats, head):
        at = 2 * SPLIT * head
        total = (stats[at + 2 : at + 3] + stats[at + 1 : at + 2]) + stats[at : at + 1]
        top = (stats[at + 5 : at + 6] + stats[at + 4 : at + 5]) + stats[at + 3 : at + 4]
        return total, top

    for head in range(heads):
        held = slice(head * HEAD_SIZE, (head + 1) * HEAD_SIZE)
        near_total, near_top = stats_of(near_stats, head)
        far_total, far_top = stats_of(far_stats, head)
        far_top = jnp.where(has_far, far_top, least_top)
        best = jnp.maximum(near_top, far_top)
        near = jnp.exp2((near_top - best) * FACTOR)
        far = jnp.exp2((far_top - best) * FACTOR)
        total = near * near_total + far * far_total
        sums = near_ref[held] * near + far_ref[held].astype(jnp.float32) * far
        o_ref[:, held] = (sums / total).astype(jnp.bfloat16).T


def step(offsets, before, roles, last, tables, columns, singles, state):
    rows = columns[0].shape[1] // 2
    heads = state[0].shape[1] // HEAD_SIZE if not before else state[0].shape[1]
    held = ALL_OFFSETS if last else offsets
    parts = [columns[offset] for offset in held if offset != FAR]
    parts += singles if FAR in held else []
    smem = pl.BlockSpec(memory_space=pltpu.SMEM)
    vmem = pl.BlockSpec(memory_space=pltpu.VMEM)
    task_count = 2 * PLANE
    scratch = [
        pltpu.VMEM((2, 2 * rows, HEAD_SIZE), jnp.bfloat16),
        pltpu.VMEM((SUM_ROWS, rows), jnp.bfloat16),
        pltpu.SMEM((task_count,), jnp.int32),
        pltpu.SMEM((task_count,), jnp.int32),
        pltpu.SMEM((task_count,), jnp.int32),
        pltpu.VMEM((rows, rows), jnp.float32),
        pltpu.VMEM((heads, rows, rows), jnp.float32),
        pltpu.VMEM((heads, rows, rows), jnp.bfloat16),
    ]
    state_shapes = ((2, heads, SUM_ROWS, rows), (2, heads, 1, rows))
    out_shape = [jax.ShapeDtypeStruct(shape, jnp.float32) for shape in state_shapes]
    inputs = (*tables, *parts, *state)
    aliases = {len(inputs) - 2: 0, len(inputs) - 1: 1}
    if last:
        scratch += [pltpu.VMEM(shape, jnp.float32) for shape in state_shapes]
        out_type = jnp.float32 if roles == (OWN,) else jnp.bfloat16
        out_shape, aliases = [jax.ShapeDtypeStruct((heads * HEAD_SIZE + STAT_ROWS, rows), out_type)], {}
    elif not before:
        out_shape.insert(0, jax.ShapeDtypeStruct((2, heads, HEAD_SIZE, rows), jnp.bfloat16))
        aliases = {}
    scratch += [pltpu.SemaphoreType.DMA((2,))]
    tasks = len(offsets) * len(roles) * 2
    out = pl.pallas_call(
        functools.partial(step_kernel, offsets, before, roles, last, held),
        out_shape=out_shape,
        in_specs=[smem, smem] + [pl.BlockSpec(memory_space=pl.ANY)] * len(parts) + [vmem] * len(state),
        out_specs=[vmem] * len(out_shape),
        scratch_shapes=scratch,
        input_output_aliases=aliases,
        compiler_params=pltpu.CompilerParams(vmem_limit_bytes=24 * 1024 * 1024),
        cost_estimate=pl.CostEstimate(
            flops=tasks * heads * rows * rows * HEAD_SIZE * 4,
            bytes_accessed=tasks * rows * HEAD_SIZE * 4,
            transcendentals=tasks * heads * rows * rows,
        ),
        name="blocks_" + "".join(str(offset) for offset in offsets) + "_role" + "".join(str(role) for role in roles),
    )(*inputs)
    if last:
        return out[0]
    return tuple(out) if not before else (state[0], *out)


def moved(value, dx, dy, dz, from_planes=range(X)):
    pairs = [
        (((x - dx) % X * Y + (y - dy) % Y) * Z + (z - dz) % Z, (x * Y + y) * Z + z)
        for x in range(X) for y in range(Y) for z in range(Z)
        if (x - dx) % X in from_planes
    ]
    return lax.ppermute(value, "seq", pairs)


def body(queries, keys, values, doc_ids, block_class):
    tables = (block_class, doc_ids.reshape(-1, DOC_STEP)[:, 0])
    both = jnp.concatenate([keys, values], axis=0)
    column = jnp.stack([both] + [moved(both, 0, dy, 0) for dy in range(1, Y)])
    single = moved(both, 0, 0, FAR)
    column, single = lax.optimization_barrier((column, single))
    far_queries = moved(queries, 1, 0, 0)
    columns = {0: column, 1: moved(column, 0, 0, 1), 7: moved(column, 0, 0, -1)}
    singles = [single] + [moved(single, 0, dy, 0) for dy in range(1, Y)]
    both_roles = (OWN, PARTNER)

    state = step((0,), (), both_roles, False, tables, columns, singles, (queries, far_queries))
    columns[1], numerators, tops = lax.optimization_barrier((columns[1], *state[1:]))
    columns[7], numerators, tops = lax.optimization_barrier((columns[7], numerators, tops))
    columns[2], columns[6] = moved(columns[1], 0, 0, 1), moved(columns[7], 0, 0, -1)
    state = step((1, 7), (0,), both_roles, False, tables, columns, singles, (state[0], numerators, tops))
    columns[2], numerators, tops = lax.optimization_barrier((columns[2], *state[1:]))
    columns[6], *singles, numerators, tops = lax.optimization_barrier((columns[6], *singles, numerators, tops))
    columns[3], columns[5] = moved(columns[2], 0, 0, 1), moved(columns[6], 0, 0, -1)
    state = step((2, 6, FAR), (0, 1, 7), both_roles, False, tables, columns, singles, (state[0], numerators, tops))
    columns[3], columns[5], numerators, tops = lax.optimization_barrier((columns[3], columns[5], *state[1:]))
    state = (state[0], numerators, tops)
    partner = step((3, 5), (0, 1, 7, 2, 6, FAR), (PARTNER,), True, tables, columns, singles, state)
    partner = moved(partner, 1, 0, 0, (0,))
    own = step((1, 7, 2, 6, FAR, 3, 5), (0,), (OWN,), True, tables, columns, singles, state)
    vmem = pl.BlockSpec(memory_space=pltpu.VMEM)
    return pl.pallas_call(
        merge_kernel,
        out_shape=jax.ShapeDtypeStruct(queries.shape, queries.dtype),
        in_specs=[vmem] * 2,
        out_specs=vmem,
        compiler_params=pltpu.CompilerParams(vmem_limit_bytes=24 * 1024 * 1024),
        name="merge",
    )(own, partner)


def solution(mesh):
    in_specs = (
        P(("dp", "seq"), "head"),
        P(("dp", "seq"), "head"),
        P(("dp", "seq"), "head"),
        P("dp"),
        P("dp", None),
    )
    out_specs = P(("dp", "seq"), "head")
    return jax.shard_map(body, mesh=mesh, in_specs=in_specs, out_specs=out_specs, check_vma=False)
```
